256 devices in a mesh: dp: 8 (over y_hi, x), pipe: 2 (over y_lo), tensor: 16 (over z, core).
Axes of the slice: x: 4, y: 4 (y_hi: 2, y_lo: 2; y = y_hi * 2 + y_lo), z: 8, core: 2. Of those that a mesh axis runs over, the one named last changes fastest.
Arguments:
- inputs: bfloat16 [2, 512, 8192], P(None, ('dp', 'tensor')), may hold values from -6 to 6
- positions: int32 [2, 512], P(None, 'dp'), may hold values from 0 to 63, as said below
- out_grads: bfloat16 [2, 512, 8192], P(None, ('dp', 'tensor')), may hold values from -6 to 6
- query_weight: bfloat16 [2, 8192, 4096], P('pipe', 'dp', 'tensor'), may hold values from -0.0625 to 0.0625
- key_value_weight: bfloat16 [2, 8192, 1024], P('pipe', 'dp', 'tensor'), may hold values from -0.0625 to 0.0625
- out_weight: bfloat16 [2, 4096, 8192], P('pipe', 'tensor', 'dp'), may hold values from -0.09375 to 0.09375
- query_stale: float32 [2, 8192, 4096], P('pipe', 'dp', 'tensor'), may hold values from -0.0625 to 0.0625
- key_value_previous_gradient: float32 [2, 8192, 1024], P('pipe', 'dp', 'tensor'), may hold values from -0.0625 to 0.0625
- out_stale: float32 [2, 4096, 8192], P('pipe', 'tensor', 'dp'), may hold values from -0.09375 to 0.09375
Outputs:
- section_outputs: bfloat16 [2, 2, 512, 8192], P('pipe', None, ('dp', 'tensor'))
- input_grads: bfloat16 [2, 2, 512, 8192], P('pipe', None, ('dp', 'tensor'))
- query_new: bfloat16 [2, 8192, 4096], P('pipe', 'dp', 'tensor')
- kv_new: bfloat16 [2, 8192, 1024], P('pipe', 'dp', 'tensor')
- out_new: bfloat16 [2, 4096, 8192], P('pipe', 'tensor', 'dp')
- query_grad: float32 [2, 8192, 4096], P('pipe', 'dp', 'tensor')
- kv_grad: float32 [2, 8192, 1024], P('pipe', 'dp', 'tensor')
- out_grad: float32 [2, 4096, 8192], P('pipe', 'tensor', 'dp')
The draws below stay inside these ranges and needn't reach their ends.
Inputs may be any that keep to these rules, and one draw needn't show every extreme that they name: In each block of 64 tokens of a micro-batch, positions rise by one from token to token and fall back to 0 where a new document starts; every block begins at 0, and the first block of micro-batch 0 is one document.
All inputs are finite; a program needn't handle non-finite values.
Results may differ from the reference program's by a relative error of at most 0.035.
Values may be sent and summed in bfloat16 or wider, within the bound.
No kernel may reach another device: no remote copies, remote signals or barrier semaphores. Data moves between devices by JAX's collectives and lax.ppermute only.
A program may use at most 128 MiB of HBM per device.

```python
import math
import jax
import jax.numpy as jnp
import numpy as np
from jax import lax

MODEL_WIDTH = 8192
HQ = 32
KEY_VALUE_HEADS = 4
HEAD_SIZE = 128
MICRO = 2
MB = 64
TOKENS = 512
N_DP = 8
N_TENSOR = 16


def draw_positions(key, part):
    key = jax.random.fold_in(key, 11)
    index = jnp.arange(TOKENS, dtype=jnp.int32)
    within = index % MB
    cuts = jax.random.randint(key, (MICRO, TOKENS), 0, 16) == 0
    whole = (jnp.arange(MICRO, dtype=jnp.int32)[:, None] == 0) & (index[None, :] < MB)
    starts = cuts & jnp.logical_not(whole) | (within[None, :] == 0)
    begin = lax.cummax(jnp.where(starts, index[None, :], 0), axis=1)
    return (index[None, :] - begin).astype(jnp.int32)


def levels(rng, dims, pieces, least, top_value):
    loudness = 1.0
    for position, blocks in pieces:
        steps = jax.random.uniform(jax.random.fold_in(jax.random.fold_in(rng, 6), position), (blocks,), jnp.float32, least / len(pieces), top_value / len(pieces))
        loudness = loudness * jnp.repeat(jnp.exp(steps), dims[position] // blocks).reshape((-1,) + (1,) * (len(dims) - 1 - position))
    return loudness


def gaussian(own_key, dims, width, most, split=(), kind=jnp.bfloat16):
    drawn = jax.random.normal(own_key, dims, jnp.float32) * width
    if len(split) > 0:
        drawn = levels(own_key, dims, split, -0.22, 0.18) * drawn
    return jnp.clip(drawn, min=-most, max=most).astype(kind)


def setup_inputs(seed: int = 0) -> dict:
    key_list = jax.random.split(jax.random.key(seed), 10)
    inputs = gaussian(key_list[0], (MICRO, TOKENS, MODEL_WIDTH), 1.0, 6.0, ((1, 128),))
    positions = draw_positions(jax.random.fold_in(key_list[9], 71), 0)
    out_grads = gaussian(key_list[2], (MICRO, TOKENS, MODEL_WIDTH), 1.0, 6.0, ((1, 128),))
    query_weight = gaussian(key_list[3], (2, MODEL_WIDTH, HQ * HEAD_SIZE), MODEL_WIDTH ** -0.5, 0.0625, ((0, 2), (1, 8), (2, 16)))
    key_value_weight = gaussian(key_list[4], (2, MODEL_WIDTH, 2 * KEY_VALUE_HEADS * HEAD_SIZE), MODEL_WIDTH ** -0.5, 0.0625, ((0, 2), (1, 8), (2, 16)))
    out_weight = gaussian(key_list[5], (2, HQ * HEAD_SIZE, MODEL_WIDTH), (HQ * HEAD_SIZE) ** -0.5, 0.09375, ((0, 2), (1, 16), (2, 8)))
    query_stale = gaussian(key_list[6], (2, MODEL_WIDTH, HQ * HEAD_SIZE), MODEL_WIDTH ** -0.5, 0.0625, ((0, 2), (1, 8), (2, 16)), jnp.float32)
    key_value_previous_gradient = gaussian(key_list[7], (2, MODEL_WIDTH, 2 * KEY_VALUE_HEADS * HEAD_SIZE), MODEL_WIDTH ** -0.5, 0.0625, ((0, 2), (1, 8), (2, 16)), jnp.float32)
    out_stale = gaussian(key_list[8], (2, HQ * HEAD_SIZE, MODEL_WIDTH), (HQ * HEAD_SIZE) ** -0.5, 0.09375, ((0, 2), (1, 16), (2, 8)), jnp.float32)
    return dict(inputs=inputs, positions=positions, out_grads=out_grads, query_weight=query_weight, key_value_weight=key_value_weight, out_weight=out_weight, query_stale=query_stale, key_value_previous_gradient=key_value_previous_gradient, out_stale=out_stale)


EPS = 1e-05
THETA = 500000.0
LR = 0.5

def saved_state(values):
    return lax.optimization_barrier(values.astype(jnp.bfloat16)).astype(jnp.float32)

def rms_scale(rows):
    return rows * lax.rsqrt(lax.optimization_barrier(jnp.mean(rows * rows, axis=-1, keepdims=True)) + EPS)

def rotate(values, positions, sign):
    half = values.shape[-1] // 2
    freqs = THETA ** (-2.0 * jnp.arange(half, dtype=jnp.float32) / values.shape[-1])
    angles = positions.astype(jnp.float32)[:, None] * freqs[None, :]
    cosine = jnp.cos(angles)[:, None, :]
    sine = sign * jnp.sin(angles)[:, None, :]
    first = values[..., :half]
    second = values[..., half:]
    return jnp.concatenate([first * cosine - second * sine, second * cosine + first * sine], axis=-1)

def visible_keys(positions):
    index = jnp.arange(positions.shape[0], dtype=jnp.int32)
    lowest = index - positions.astype(jnp.int32)
    return (index[None, :] <= index[:, None]) & (index[None, :] >= lowest[:, None])

def attend(queries, keys, values, visible):
    scores = jnp.einsum('qgh,kh->gqk', queries, keys, precision=lax.Precision.HIGHEST) / math.sqrt(queries.shape[-1])
    scores = jnp.where(visible[None], scores, -1e+30)
    weights = jnp.exp(scores)
    probs = weights / lax.optimization_barrier(jnp.sum(weights, axis=-1, keepdims=True))
    probs = probs + lax.stop_gradient(saved_state(probs) - probs)
    return jnp.einsum('gqk,kh->qgh', probs, values, precision=lax.Precision.HIGHEST)

def project(normalized_rows, positions, query_weight, key_value_weight):
    token_list = normalized_rows.shape[0]
    query_proj = jnp.dot(normalized_rows, query_weight, preferred_element_type=jnp.float32)
    key_value_projected = saved_state(jnp.dot(normalized_rows, key_value_weight, preferred_element_type=jnp.float32)).reshape(token_list, KEY_VALUE_HEADS, 2, HEAD_SIZE)
    keys = saved_state(rotate(key_value_projected[:, :, 0], positions, 1.0))
    queries = saved_state(rotate(query_proj.reshape(token_list, HQ, HEAD_SIZE), positions, 1.0))
    return (queries, keys, key_value_projected[:, :, 1])

def by_group(queries, keys, values):
    owning_section = np.arange(N_TENSOR) * KEY_VALUE_HEADS // N_TENSOR
    grouped = queries.reshape(queries.shape[0], N_TENSOR, HQ // N_TENSOR, HEAD_SIZE)
    return (grouped, keys[:, owning_section], values[:, owning_section])

def group_attend(grouped, keys, values, visible):
    return jax.vmap(attend, in_axes=(1, 1, 1, None), out_axes=1)(grouped, keys, values, visible)

def section_forward(inputs, positions, query_weight, key_value_weight, out_weight):
    token_list = inputs.shape[0]
    normalized_rows = rms_scale(inputs.astype(jnp.float32)).astype(jnp.bfloat16)
    queries, keys, values = project(normalized_rows, positions, query_weight, key_value_weight)
    grouped, group_keys, group_values = by_group(queries, keys, values)
    weighted = group_attend(grouped, group_keys, group_values, visible_keys(positions))
    mixed = weighted.reshape(token_list, HQ * HEAD_SIZE).astype(jnp.bfloat16)
    partial_value = jnp.einsum('mrc,rcd->rmd', mixed.astype(jnp.float32).reshape(token_list, N_TENSOR, -1), out_weight.astype(jnp.float32).reshape(N_TENSOR, -1, MODEL_WIDTH), precision=lax.Precision.HIGHEST)
    reduced = lax.optimization_barrier(jnp.sum(saved_state(partial_value), axis=0))
    return (inputs.astype(jnp.float32) + reduced).astype(jnp.bfloat16)

def section_backward(inputs, positions, query_weight, key_value_weight, out_weight, grad_out):
    token_list = inputs.shape[0]
    normed_wide, norm_pull = jax.vjp(rms_scale, inputs.astype(jnp.float32))
    normalized_rows = normed_wide.astype(jnp.bfloat16)
    queries, keys, values = project(normalized_rows, positions, query_weight, key_value_weight)
    grouped, group_keys, group_values = by_group(queries, keys, values)
    visible = visible_keys(positions)
    weighted, pullback = jax.vjp(lambda first, second, third: group_attend(first, second, third, visible), grouped, group_keys, group_values)
    mixed = weighted.reshape(token_list, HQ * HEAD_SIZE).astype(jnp.bfloat16)
    d_mixed = jnp.dot(grad_out, out_weight.T, preferred_element_type=jnp.float32).reshape(grouped.shape)
    d_query, d_key, d_value = pullback(d_mixed)
    dq_proj = rotate(d_query.reshape(token_list, HQ, HEAD_SIZE), positions, -1.0).reshape(token_list, HQ * HEAD_SIZE).astype(jnp.bfloat16)
    group_share = jnp.stack([rotate(d_key, positions, -1.0), d_value], axis=2)
    head_share = lax.optimization_barrier(jnp.sum(saved_state(group_share).reshape(token_list, KEY_VALUE_HEADS, N_TENSOR // KEY_VALUE_HEADS, 2, HEAD_SIZE), axis=2))
    key_value_gradient = head_share.reshape(token_list, 2 * KEY_VALUE_HEADS * HEAD_SIZE).astype(jnp.bfloat16)
    partial_value = jnp.einsum('mrc,drc->rmd', dq_proj.astype(jnp.float32).reshape(token_list, N_TENSOR, -1), query_weight.astype(jnp.float32).reshape(MODEL_WIDTH, N_TENSOR, -1), precision=lax.Precision.HIGHEST)
    partial_value = partial_value + jnp.einsum('mrc,drc->rmd', key_value_gradient.astype(jnp.float32).reshape(token_list, N_TENSOR, -1), key_value_weight.astype(jnp.float32).reshape(MODEL_WIDTH, N_TENSOR, -1), precision=lax.Precision.HIGHEST)
    d_normed = lax.optimization_barrier(jnp.sum(saved_state(partial_value), axis=0))
    d_inputs = (grad_out.astype(jnp.float32) + norm_pull(d_normed)[0]).astype(jnp.bfloat16)
    grad_q = jnp.dot(normalized_rows.T, dq_proj, preferred_element_type=jnp.float32)
    grad_kv = jnp.dot(normalized_rows.T, key_value_gradient, preferred_element_type=jnp.float32)
    grad_o = jnp.dot(mixed.T, grad_out, preferred_element_type=jnp.float32)
    return (d_inputs, (grad_q, grad_kv, grad_o))

def reference(inputs, positions, out_grads, query_weight, key_value_weight, out_weight, query_stale, key_value_previous_gradient, out_stale):
    query_new = (query_weight.astype(jnp.float32) - LR * query_stale).astype(jnp.bfloat16)
    kv_new = (key_value_weight.astype(jnp.float32) - LR * key_value_previous_gradient).astype(jnp.bfloat16)
    out_new = (out_weight.astype(jnp.float32) - LR * out_stale).astype(jnp.bfloat16)
    blocks = inputs.reshape(MICRO, N_DP, MB, MODEL_WIDTH).transpose(1, 0, 2, 3)
    spots = positions.reshape(MICRO, N_DP, MB).transpose(1, 0, 2)
    cotangents = out_grads.reshape(MICRO, N_DP, MB, MODEL_WIDTH).transpose(1, 0, 2, 3)

    def replica(totals, data):
        block, spot, cotangent = data
        first_outs, second_outs, first_backs, second_backs = ([], [], [], [])
        sums = [None, None]
        for micro in range(MICRO):
            first_out = section_forward(block[micro], spot[micro], query_new[0], kv_new[0], out_new[0])
            second_out = section_forward(first_out, spot[micro], query_new[1], kv_new[1], out_new[1])
            second_back, second_grads = section_backward(first_out, spot[micro], query_new[1], kv_new[1], out_new[1], cotangent[micro])
            first_back, first_grads = section_backward(block[micro], spot[micro], query_new[0], kv_new[0], out_new[0], second_back)
            first_outs.append(first_out)
            second_outs.append(second_out)
            first_backs.append(first_back)
            second_backs.append(second_back)
            for section, grads in enumerate((first_grads, second_grads)):
                if sums[section] is None:
                    sums[section] = grads
                else:
                    sums[section] = tuple((older + newer for older, newer in zip(sums[section], grads)))
        stacked = tuple((jnp.stack([saved_state(sums[0][member]), saved_state(sums[1][member])]) for member in range(3)))
        totals = tuple((total + extra for total, extra in zip(totals, stacked)))
        return (totals, (jnp.stack(first_outs), jnp.stack(second_outs), jnp.stack(first_backs), jnp.stack(second_backs)))
    zeros = (jnp.zeros(query_new.shape, jnp.float32), jnp.zeros(kv_new.shape, jnp.float32), jnp.zeros(out_new.shape, jnp.float32))
    totals, results = lax.scan(replica, zeros, (blocks, spots, cotangents))

    def unblock(values):
        return values.transpose(1, 0, 2, 3).reshape(MICRO, TOKENS, MODEL_WIDTH)
    section_outputs = jnp.stack([unblock(results[0]), unblock(results[1])])
    input_grads = jnp.stack([unblock(results[2]), unblock(results[3])])
    return (section_outputs, input_grads, query_new, kv_new, out_new, totals[0], totals[1], totals[2])
```

```python
import math

import jax
import jax.numpy as jnp
from jax import lax
from jax.sharding import PartitionSpec as P

HEAD_SIZE = 128
EPS = 1e-05
THETA = 500000.0
LR = 0.5
BF = jnp.bfloat16
F32 = jnp.float32


def mm(a, b, ca=1, cb=0):
    return lax.dot_general(a, b, (((ca,), (cb,)), ((), ())), preferred_element_type=F32)


def swap(value, axis, mask):
    pairs = [(source, source ^ mask) for source in range(lax.axis_size(axis))]
    return lax.ppermute(value, axis, pairs)


def same_core(size):
    return [list(range(c, size, 2)) for c in range(2)]


def z_exchange(value):
    size = lax.axis_size("tensor")
    return lax.all_to_all(
        value, "tensor", 0, 0, axis_index_groups=same_core(size), tiled=True
    )


def dp_exchange(value):
    return lax.all_to_all(value, "dp", 0, 0, tiled=True)


def tile_rows(value, copies):
    return jnp.broadcast_to(value[None], (copies,) + value.shape).reshape(
        (copies * value.shape[0],) + value.shape[1:]
    )


def gather_z(rows, nz):
    mine = z_exchange(tile_rows(rows, nz))
    return mine, swap(mine, "tensor", 1)


def scatter_z(part_mine, part_other, nz):
    moved = swap(part_other.astype(BF), "tensor", 1)
    pair = (part_mine + moved.astype(F32)).astype(BF)
    got = z_exchange(pair)
    return jnp.sum(got.reshape((nz, -1) + got.shape[1:]).astype(F32), axis=0)


def gather_dp(rows, n):
    return dp_exchange(tile_rows(rows, n))


def scatter_dp(part, n):
    got = dp_exchange(part)
    return jnp.sum(got.reshape((n, -1) + got.shape[1:]).astype(F32), axis=0)


def rotate(values, cosine, sine):
    half = values.shape[-1] // 2
    first = values[..., :half]
    second = values[..., half:]
    return jnp.concatenate(
        [first * cosine - second * sine, second * cosine + first * sine], axis=-1
    )


def split_pair(column):
    high = column.astype(BF)
    low = (column - high.astype(F32)).astype(BF)
    wide = jnp.zeros((column.shape[0], 126), BF)
    return jnp.concatenate([high[:, None], low[:, None], wide], axis=1)


def attention(q_raw, kv_raw, total, width, cosine, sine, visible):
    scale = lax.rsqrt(total / width + EPS)[:, None]
    tokens = q_raw.shape[0]
    heads = q_raw.shape[1] // HEAD_SIZE
    q = (q_raw * scale).reshape(tokens, heads, HEAD_SIZE)
    queries = rotate(q, cosine[:, None], sine[:, None]).astype(BF)
    kv = (kv_raw * scale).astype(BF)
    keys = rotate(kv[:, :HEAD_SIZE].astype(F32), cosine, sine).astype(BF)
    values = kv[:, HEAD_SIZE:]
    scores = jnp.einsum("qgh,kh->gqk", queries, keys, preferred_element_type=F32) / math.sqrt(
        HEAD_SIZE
    )
    scores = jnp.where(visible[None], scores, -1e30)
    weights = jnp.exp(scores)
    probs = weights / jnp.sum(weights, axis=-1, keepdims=True)
    low = probs.astype(BF)
    mixed = jnp.einsum("gqk,kh->qgh", low, values, preferred_element_type=F32)
    mixed = mixed.reshape(tokens, -1).astype(BF)
    return mixed, (q_raw, kv_raw, scale, queries, keys, values, probs, low)


def attention_back(saved, d_mixed, width, cosine, sine):
    q_raw, kv_raw, scale, queries, keys, values, probs, low = saved
    tokens = q_raw.shape[0]
    dm = d_mixed.astype(BF).reshape(queries.shape)
    d_probs = jnp.einsum("qgh,kh->gqk", dm, values, preferred_element_type=F32)
    d_values = jnp.einsum("gqk,qgh->kh", low, dm, preferred_element_type=F32)
    d_scores = probs * (d_probs - jnp.sum(probs * d_probs, axis=-1, keepdims=True))
    d_scores = (d_scores / math.sqrt(HEAD_SIZE)).astype(BF)
    d_queries = jnp.einsum("gqk,kh->qgh", d_scores, keys, preferred_element_type=F32)
    d_keys = jnp.einsum("gqk,qgh->kh", d_scores, queries, preferred_element_type=F32)
    dq = rotate(d_queries, cosine[:, None], -sine[:, None]).reshape(tokens, -1)
    dkv = jnp.concatenate([rotate(d_keys, cosine, -sine), d_values], axis=1)
    dq = (dq * scale).astype(BF)
    dkv = (dkv * scale).astype(BF)
    dot = jnp.sum(dq.astype(F32) * q_raw, axis=1) + jnp.sum(dkv.astype(F32) * kv_raw, axis=1)
    coef = dot * scale[:, 0] * scale[:, 0] / width
    return dq, dkv, coef


def shards(
    inputs,
    positions,
    out_grads,
    query_weight,
    key_value_weight,
    out_weight,
    query_stale,
    key_value_previous_gradient,
    out_stale,
):
    n_dp = lax.axis_size("dp")
    ranks = lax.axis_size("tensor")
    nz = ranks // 2
    pipe = lax.axis_index("pipe")
    rank = lax.axis_index("tensor")
    core = rank % 2
    first = pipe == 0
    micro, own, width = inputs.shape
    feats = width // n_dp
    block = own * ranks
    tokens = block * n_dp
    half = tokens // 2

    query_new = (query_weight.astype(F32) - LR * query_stale).astype(BF)
    kv_new = (key_value_weight.astype(F32) - LR * key_value_previous_gradient).astype(BF)
    out_new = (out_weight.astype(F32) - LR * out_stale).astype(BF)

    def both(own_part):
        other = swap(own_part, "pipe", 1)
        return jnp.where(first, own_part, other), jnp.where(first, other, own_part)

    wq0, wq1 = both(query_new[0])
    wo0, wo1 = both(out_new[0])
    kv_own = kv_new[0].T
    kv_side = swap(kv_own, "tensor", 1)
    kv_pair = jnp.where(
        core == 0,
        jnp.concatenate([kv_own, kv_side], axis=0),
        jnp.concatenate([kv_side, kv_own], axis=0),
    )
    kv_far = swap(kv_pair, "tensor", 2)
    even = (rank // 2) % 2 == 0
    kv_full = jnp.where(
        even,
        jnp.concatenate([kv_pair, kv_far], axis=0),
        jnp.concatenate([kv_far, kv_pair], axis=0),
    )
    wkv0, wkv1 = both(kv_full)

    b_row = lax.broadcasted_iota(jnp.int32, (tokens, tokens), 0)
    c_row = lax.broadcasted_iota(jnp.int32, (tokens, tokens), 1)

    def block_major(rel_core, chip, rest):
        return (rest // own) * block + (chip * 2 + rel_core) * own + rest % own

    rel = (c_row // half) ^ core
    inside = c_row % half
    order_c = (b_row == block_major(rel, inside // (n_dp * own), inside % (n_dp * own))).astype(BF)
    rk = c_row // (n_dp * own)
    order_r = (b_row == block_major(rk % 2, rk // 2, c_row % (n_dp * own))).astype(BF)

    spots = lax.dynamic_index_in_dim(positions, pipe, 0, keepdims=False)
    freqs = THETA ** (-2.0 * jnp.arange(HEAD_SIZE // 2, dtype=F32) / HEAD_SIZE)
    angles = spots.astype(F32)[:, None] * freqs[None, :]
    cosine = jnp.cos(angles)
    sine = jnp.sin(angles)
    index = jnp.arange(block, dtype=jnp.int32)
    visible = (index[None, :] <= index[:, None]) & (index[None, :] >= (index - spots)[:, None])

    start = jnp.stack(
        [
            lax.dynamic_index_in_dim(inputs, pipe, 0, keepdims=False),
            lax.dynamic_index_in_dim(out_grads, pipe, 0, keepdims=False),
        ]
    )
    start = start.reshape(2, own, n_dp, feats).transpose(2, 0, 1, 3).reshape(n_dp * 2 * own, feats)
    start = dp_exchange(start).reshape(n_dp, 2, own, feats)
    h0 = start[:, 0].reshape(n_dp * own, feats)
    g1 = start[:, 1].reshape(n_dp * own, feats)

    big_g1 = lax.all_gather(g1, "tensor", axis=0, tiled=True)

    def project(rows, wq, wkv):
        wide = rows.astype(F32)
        q = mm(rows, wq)
        kv = mm(rows, wkv, 1, 1)
        return jnp.concatenate(
            [q.astype(BF), kv.astype(BF), split_pair(jnp.sum(wide * wide, axis=1))], axis=1
        )

    def to_blocks(part):
        return mm(order_c, part).astype(BF)

    nq = query_new.shape[2]
    nkv = 2 * HEAD_SIZE

    def unpack(total):
        return (
            total[:, :nq],
            total[:, nq : nq + nkv],
            total[:, nq + nkv] + total[:, nq + nkv + 1],
        )

    h0_mine, h0_other = gather_z(h0, nz)
    part = jnp.concatenate([project(h0_mine, wq0, wkv0), project(h0_other, wq0, wkv0)], axis=0)
    total = scatter_dp(to_blocks(part), n_dp)
    mixed0, saved0 = attention(*unpack(total), width, cosine, sine, visible)
    all_m0 = mm(order_c, gather_dp(mixed0, n_dp), 0, 0).astype(BF)
    reduced = scatter_z(mm(all_m0[:half], wo0), mm(all_m0[half:], wo0), nz)
    h1 = (h0.astype(F32) + reduced).astype(BF)

    dm1 = mm(order_r, mm(big_g1, wo1, 1, 1).astype(BF)).astype(BF)
    h1_mine, h1_other = gather_z(h1, nz)
    part = jnp.concatenate([project(h1_mine, wq1, wkv1), project(h1_other, wq1, wkv1)], axis=0)
    total = scatter_dp(jnp.concatenate([to_blocks(part), dm1], axis=1), n_dp)
    packed = nq + nkv + 128
    mixed1, saved1 = attention(*unpack(total[:, :packed]), width, cosine, sine, visible)
    dq1, dkv1, coef1 = attention_back(saved1, total[:, packed:], width, cosine, sine)

    def back(dq, dkv, coef, extra, mine, other, wq, wkv, grad_rows):
        sent = jnp.concatenate([dq, dkv, split_pair(coef)] + extra, axis=1)
        got = gather_dp(sent, n_dp)
        rows = mm(order_c, got[:, : nq + nkv + 128], 0, 0).astype(BF)
        all_q = rows[:, :nq]
        all_kv = rows[:, nq : nq + nkv]
        c = rows[:, nq + nkv].astype(F32) + rows[:, nq + nkv + 1].astype(F32)

        def term(lo, hi, held):
            value = mm(all_q[lo:hi], wq, 1, 1) + mm(all_kv[lo:hi], wkv)
            return value - held.astype(F32) * c[lo:hi, None]

        reduced = scatter_z(term(0, half, mine), term(half, tokens, other), nz)
        grad = (grad_rows.astype(F32) + reduced).astype(BF)
        grad_q = mm(mine, all_q[:half], 0, 0) + mm(other, all_q[half:], 0, 0)
        grad_kv = mm(all_kv[:half], mine, 0, 0) + mm(all_kv[half:], other, 0, 0)
        return grad, grad_q, grad_kv, got[:, nq + nkv + 128 :]

    g0, gq1, gkv1, got_m1 = back(dq1, dkv1, coef1, [mixed1], h1_mine, h1_other, wq1, wkv1, g1)
    all_m1 = mm(order_r, got_m1, 0, 0).astype(BF)
    go1 = mm(all_m1, big_g1, 0, 0)
    out1 = lax.psum_scatter(
        mm(all_m1, wo1).astype(BF), "tensor", scatter_dimension=0, tiled=True
    )
    h2 = (h1.astype(F32) + out1.astype(F32)).astype(BF)

    g0_mine, g0_other = gather_z(g0, nz)
    dm0 = jnp.concatenate([mm(g0_mine, wo0, 1, 1), mm(g0_other, wo0, 1, 1)], axis=0).astype(BF)
    d_mixed0 = scatter_dp(mm(order_c, dm0).astype(BF), n_dp)
    dq0, dkv0, coef0 = attention_back(saved0, d_mixed0, width, cosine, sine)
    go0 = mm(all_m0[:half], g0_mine, 0, 0) + mm(all_m0[half:], g0_other, 0, 0)
    gi, gq0, gkv0, _ = back(dq0, dkv0, coef0, [], h0_mine, h0_other, wq0, wkv0, g0)

    def kv_columns(grad):
        cols = grad.shape[0] // 4
        quarters = grad.astype(BF).reshape(2, 2, cols, feats)
        keep = lax.dynamic_index_in_dim(quarters, core, 1, keepdims=False)
        send = lax.dynamic_index_in_dim(quarters, 1 - core, 1, keepdims=False)
        pair = keep.astype(F32) + swap(send, "tensor", 1).astype(F32)
        pair = pair.astype(BF)
        zz = (rank // 2) % 2
        keep = lax.dynamic_index_in_dim(pair, zz, 0, keepdims=False)
        send = lax.dynamic_index_in_dim(pair, 1 - zz, 0, keepdims=False)
        return keep.astype(F32) + swap(send, "tensor", 2).astype(F32)

    def home(grad0, grad1):
        to1 = lax.ppermute(grad1.astype(BF), "pipe", [(0, 1)])
        to0 = lax.ppermute(grad0.astype(BF), "pipe", [(1, 0)])
        return jnp.where(first, grad0 + to0.astype(F32), grad1 + to1.astype(F32))

    query_grad = home(gq0, gq1)
    kv_grad = home(kv_columns(gkv0), kv_columns(gkv1)).T
    out_grad = home(go0, go1)

    ends = jnp.stack([h1, gi, h2, g0]).reshape(4, n_dp, own, feats).transpose(1, 0, 2, 3)
    ends = dp_exchange(ends.reshape(n_dp * 4 * own, feats)).reshape(n_dp, 2, 2, own, feats)
    ends = ends.transpose(1, 2, 3, 0, 4).reshape(2, 2, own, width)
    keep = lax.dynamic_index_in_dim(ends, pipe, 0, keepdims=False)
    send = lax.dynamic_index_in_dim(ends, 1 - pipe, 0, keepdims=False)
    came = swap(send, "pipe", 1)
    rows = jnp.where(first, jnp.stack([keep, came], 1), jnp.stack([came, keep], 1))
    return (
        rows[0][None],
        rows[1][None],
        query_new,
        kv_new,
        out_new,
        query_grad[None],
        kv_grad[None],
        out_grad[None],
    )


def solution(mesh):
    placed = (
        P(None, ("dp", "tensor"), None),
        P(None, "dp"),
        P(None, ("dp", "tensor"), None),
        P("pipe", "dp", "tensor"),
        P("pipe", "dp", "tensor"),
        P("pipe", "tensor", "dp"),
        P("pipe", "dp", "tensor"),
        P("pipe", "dp", "tensor"),
        P("pipe", "tensor", "dp"),
    )
    return jax.shard_map(
        shards,
        mesh=mesh,
        in_specs=placed,
        out_specs=(
            P("pipe", None, ("dp", "tensor"), None),
            P("pipe", None, ("dp", "tensor"), None),
            P("pipe", "dp", "tensor"),
            P("pipe", "dp", "tensor"),
            P("pipe", "tensor", "dp"),
            P("pipe", "dp", "tensor"),
            P("pipe", "dp", "tensor"),
            P("pipe", "tensor", "dp"),
        ),
        check_vma=False,
    )
```

```python
import functools
import math

import jax
import jax.numpy as jnp
from jax import lax
from jax.experimental import pallas as pl
from jax.experimental.pallas import tpu as pltpu
from jax.sharding import PartitionSpec as P

HEAD_SIZE = 128
EPS = 1e-05
THETA = 500000.0
LR = 0.5
BF = jnp.bfloat16
F32 = jnp.float32


def mm(a, b, ca=1, cb=0):
    return lax.dot_general(a, b, (((ca,), (cb,)), ((), ())), preferred_element_type=F32)


def swap(value, axis, mask):
    pairs = [(source, source ^ mask) for source in range(lax.axis_size(axis))]
    return lax.ppermute(value, axis, pairs)


def same_core(size):
    return [list(range(c, size, 2)) for c in range(2)]


def z_exchange(value):
    size = lax.axis_size("tensor")
    return lax.all_to_all(
        value, "tensor", 0, 0, axis_index_groups=same_core(size), tiled=True
    )


def dp_exchange(value):
    return lax.all_to_all(value, "dp", 0, 0, tiled=True)


def tile_rows(value, copies):
    return jnp.broadcast_to(value[None], (copies,) + value.shape).reshape(
        (copies * value.shape[0],) + value.shape[1:]
    )


def call(body, shapes, *operands, flops=0):
    outs = [jax.ShapeDtypeStruct(shape, kind) for shape, kind in shapes]
    moved = sum(x.size * x.dtype.itemsize for x in list(operands) + outs)
    return pl.pallas_call(
        body,
        out_shape=outs,
        in_specs=[pl.BlockSpec(memory_space=pltpu.VMEM)] * len(operands),
        out_specs=[pl.BlockSpec(memory_space=pltpu.VMEM)] * len(outs),
        compiler_params=pltpu.CompilerParams(vmem_limit_bytes=48 * 2**20),
        cost_estimate=pl.CostEstimate(flops=flops, bytes_accessed=moved, transcendentals=0),
    )(*operands)


def one_hot(target):
    size = target.shape[1]
    row = lax.broadcasted_iota(jnp.int32, (size, size), 0)
    return jnp.where(row == target, 1.0, 0.0).astype(BF)


def pair_columns(column):
    high = column.astype(BF).astype(F32)
    lane = lax.broadcasted_iota(jnp.int32, (column.shape[0], 128), 1)
    return jnp.where(lane == 0, high, jnp.where(lane == 1, column - high, 0.0)).astype(BF)


def project_body(target, mine, other, wq, wkv, *rest):
    half = mine.shape[0]
    parts = []
    for rows in (mine[...], other[...]):
        wide = rows.astype(F32)
        squares = jnp.sum(wide * wide, axis=1, keepdims=True)
        parts.append(
            jnp.concatenate(
                [mm(rows, wq[...]).astype(BF), mm(rows, wkv[...], 1, 1).astype(BF), pair_columns(squares)],
                axis=1,
            )
        )
    order = one_hot(target[...])
    value = (mm(order[:, :half], parts[0]) + mm(order[:, half:], parts[1])).astype(BF)
    out = rest[-1]
    out[:, : value.shape[1]] = value
    if len(rest) > 1:
        out[:, value.shape[1] :] = rest[0][...]


def project(target, mine, other, wq, wkv, *extra):
    rows = 2 * mine.shape[0]
    cols = wq.shape[1] + wkv.shape[0] + 128
    flops = 2 * rows * cols * (mine.shape[1] + rows)
    cols = cols + sum(x.shape[1] for x in extra)
    return call(
        project_body, [((rows, cols), BF)], target, mine, other, wq, wkv, *extra, flops=flops
    )[0]


def mixed_grad_body(target, *refs):
    wo, out = refs[-2:]
    order = one_hot(target[...])
    total = None
    at = 0
    for part in refs[:-2]:
        count = part.shape[0]
        low = mm(part[...], wo[...], 1, 1).astype(BF)
        value = mm(order[:, at : at + count], low)
        total = value if total is None else total + value
        at = at + count
    out[...] = total.astype(BF)


def mixed_grad(target, parts, wo):
    rows = target.shape[1]
    cols = wo.shape[0]
    flops = 2 * rows * cols * (wo.shape[1] + rows)
    return call(mixed_grad_body, [((rows, cols), BF)], target, *parts, wo, flops=flops)[0]


def whole_body(target, got, wo, rows_out, out):
    rows = mm(one_hot(target[...]), got[...], 0, 0).astype(BF)
    rows_out[...] = rows
    out[...] = mm(rows, wo[...]).astype(BF)


def whole_project(target, got, wo):
    rows, cols = got.shape
    feats = wo.shape[1]
    return call(
        whole_body,
        [((rows, cols), BF), ((rows, feats), BF)],
        target,
        got,
        wo,
        flops=2 * rows * cols * (rows + feats),
    )


def out_body(target, got, wo, rows_out, other_out, mine_out):
    half = mine_out.shape[0]
    rows = mm(one_hot(target[...]), got[...], 0, 0).astype(BF)
    rows_out[...] = rows
    other_out[...] = mm(rows[half:], wo[...]).astype(BF)
    mine_out[...] = mm(rows[:half], wo[...])


def out_project(target, got, wo):
    rows, cols = got.shape
    feats = wo.shape[1]
    return call(
        out_body,
        [((rows, cols), BF), ((rows // 2, feats), BF), ((rows // 2, feats), F32)],
        target,
        got,
        wo,
        flops=2 * rows * cols * (rows + feats),
    )


def back_body(target, got, mine, other, wq, wkv, rows_out, other_out, mine_out):
    half = mine.shape[0]
    nq = wq.shape[1]
    end = nq + wkv.shape[0]
    rows = mm(one_hot(target[...]), got[:, : end + 128], 0, 0)
    coef = jnp.sum(rows[:, end:], axis=1, keepdims=True)
    low = rows[:, :end].astype(BF)
    rows_out[...] = low

    def term(part, c, held):
        value = mm(part[:, :nq], wq[...], 1, 1) + mm(part[:, nq:], wkv[...])
        return value - held[...].astype(F32) * c

    other_out[...] = term(low[half:], coef[half:], other).astype(BF)
    mine_out[...] = term(low[:half], coef[:half], mine)


def back_project(target, got, mine, other, wq, wkv):
    rows = got.shape[0]
    cols = wq.shape[1] + wkv.shape[0]
    feats = mine.shape[1]
    return call(
        back_body,
        [((rows, cols), BF), ((rows // 2, feats), BF), ((rows // 2, feats), F32)],
        target,
        got,
        mine,
        other,
        wq,
        wkv,
        flops=2 * rows * (cols + 128) * (rows + feats),
    )


def settle_body(count, got, held, out, wide_out):
    rows = held.shape[0]
    total = held[...].astype(F32)
    for i in range(count):
        total = total + got[i * rows : (i + 1) * rows].astype(F32)
    low = total.astype(BF)
    out[...] = low
    for i in range(count):
        wide_out[i * rows : (i + 1) * rows] = low


def settle(got, held):
    count = got.shape[0] // held.shape[0]
    return call(
        functools.partial(settle_body, count),
        [(held.shape, BF), (got.shape, BF)],
        got,
        held,
    )


def turn(value, cosine, sine):
    return value * cosine + pltpu.roll(value, HEAD_SIZE // 2, 1) * sine


def heads_down(value):
    count = value.shape[1] // HEAD_SIZE
    return jnp.concatenate(
        [value[:, i * HEAD_SIZE : (i + 1) * HEAD_SIZE] for i in range(count)], axis=0
    )


def heads_across(value, tokens):
    count = value.shape[0] // tokens
    return jnp.concatenate([value[i * tokens : (i + 1) * tokens] for i in range(count)], axis=1)


def add_parts(ref, tokens):
    total = ref[:tokens].astype(F32)
    for i in range(1, ref.shape[0] // tokens):
        total = total + ref[i * tokens : (i + 1) * tokens].astype(F32)
    return total


def look(total, nq, width, cosine, sine, mask):
    tokens = total.shape[0]
    heads = nq // HEAD_SIZE
    end = nq + 2 * HEAD_SIZE
    squares = jnp.sum(total[:, end:], axis=1, keepdims=True)
    scale = lax.rsqrt(squares / width + EPS)
    wide_cos = jnp.concatenate([cosine] * heads, axis=0)
    wide_sin = jnp.concatenate([sine] * heads, axis=0)
    queries = turn(heads_down(total[:, :nq] * scale), wide_cos, wide_sin).astype(BF)
    kv = (total[:, nq:end] * scale).astype(BF)
    keys = turn(kv[:, :HEAD_SIZE].astype(F32), cosine, sine).astype(BF)
    values = kv[:, HEAD_SIZE:]
    scores = mm(queries, keys, 1, 1) * (1.0 / math.sqrt(HEAD_SIZE))
    weights = jnp.exp(jnp.where(mask > 0.0, scores, -1e30))
    probs = weights / jnp.sum(weights, axis=1, keepdims=True)
    low = probs.astype(BF)
    return scale, queries, keys, values, probs, low, wide_cos, wide_sin


def look_back(total, d_mixed, nq, width, cosine, sine, seen):
    scale, queries, keys, values, probs, low, wide_cos, wide_sin = seen
    tokens = total.shape[0]
    end = nq + 2 * HEAD_SIZE
    dm = heads_down(d_mixed).astype(BF)
    d_probs = mm(dm, values, 1, 1)
    d_values = mm(low, dm, 0, 0)
    d_scores = probs * (d_probs - jnp.sum(probs * d_probs, axis=1, keepdims=True))
    d_scores = (d_scores * (1.0 / math.sqrt(HEAD_SIZE))).astype(BF)
    dq = turn(mm(d_scores, keys), wide_cos, -wide_sin)
    dk = turn(mm(d_scores, queries, 0, 0), cosine, -sine)
    dq = (heads_across(dq, tokens) * scale).astype(BF)
    dkv = (jnp.concatenate([dk, d_values], axis=1) * scale).astype(BF)
    both = jnp.concatenate([dq, dkv], axis=1)
    dot = jnp.sum(both.astype(F32) * total[:, :end], axis=1, keepdims=True)
    return jnp.concatenate([both, pair_columns(dot * scale * scale / width)], axis=1)


def spread(out, value):
    rows = value.shape[0]
    for i in range(out.shape[0] // rows):
        out[i * rows : (i + 1) * rows] = value


def forward_body(nq, width, got, cosine, sine, mask, mixed_out, total_out):
    tokens = cosine.shape[0]
    total = add_parts(got, tokens)
    total_out[...] = total
    seen = look(total, nq, width, cosine[...], sine[...], mask[...])
    spread(mixed_out, heads_across(mm(seen[5], seen[3]), tokens).astype(BF))


def both_body(nq, width, got, cosine, sine, mask, sent_out):
    tokens = cosine.shape[0]
    total = add_parts(got, tokens)
    d_mixed = total[:, total.shape[1] - nq :]
    total = total[:, : total.shape[1] - nq]
    seen = look(total, nq, width, cosine[...], sine[...], mask[...])
    mixed = heads_across(mm(seen[5], seen[3]), tokens).astype(BF)
    sent = look_back(total, d_mixed, nq, width, cosine[...], sine[...], seen)
    spread(sent_out, jnp.concatenate([sent, mixed], axis=1))


def backward_body(nq, width, total, grads, cosine, sine, mask, sent_out):
    tokens = cosine.shape[0]
    d_mixed = add_parts(grads, tokens)
    seen = look(total[...], nq, width, cosine[...], sine[...], mask[...])
    spread(sent_out, look_back(total[...], d_mixed, nq, width, cosine[...], sine[...], seen))


def shards(
    inputs,
    positions,
    out_grads,
    query_weight,
    key_value_weight,
    out_weight,
    query_stale,
    key_value_previous_gradient,
    out_stale,
):
    n_dp = lax.axis_size("dp")
    ranks = lax.axis_size("tensor")
    nz = ranks // 2
    pipe = lax.axis_index("pipe")
    rank = lax.axis_index("tensor")
    core = rank % 2
    first = pipe == 0
    micro, own, width = inputs.shape
    feats = width // n_dp
    block = own * ranks
    tokens = block * n_dp
    half = tokens // 2

    query_new = (query_weight.astype(F32) - LR * query_stale).astype(BF)
    kv_new = (key_value_weight.astype(F32) - LR * key_value_previous_gradient).astype(BF)
    out_new = (out_weight.astype(F32) - LR * out_stale).astype(BF)

    def arrange(own_part, other):
        return jnp.where(first, own_part, other), jnp.where(first, other, own_part)

    wq0, wq1 = arrange(query_new[0], swap(query_new[0], "pipe", 1))
    kv_own = kv_new[0].T
    kv_here, kv_next = arrange(kv_own, swap(kv_own, "pipe", 1))
    even = (rank // 2) % 2 == 0

    def whole_head(own_part):
        side = swap(own_part, "tensor", 1)
        pair = jnp.where(
            core == 0,
            jnp.concatenate([own_part, side], axis=0),
            jnp.concatenate([side, own_part], axis=0),
        )
        far = swap(pair, "tensor", 2)
        return jnp.where(
            even,
            jnp.concatenate([pair, far], axis=0),
            jnp.concatenate([far, pair], axis=0),
        )

    wkv0 = whole_head(kv_here)

    at = lax.broadcasted_iota(jnp.int32, (1, tokens), 1)
    inside = at % half
    chip = inside // (n_dp * own)
    rest = inside % (n_dp * own)
    target = (rest // own) * block + (chip * 2 + ((at // half) ^ core)) * own + rest % own
    rest = at % (n_dp * own)
    by_rank = (rest // own) * block + (at // (n_dp * own)) * own + rest % own

    spots = lax.dynamic_index_in_dim(positions, pipe, 0, keepdims=False)
    freqs = THETA ** (-2.0 * jnp.arange(HEAD_SIZE // 2, dtype=F32) / HEAD_SIZE)
    angles = spots.astype(F32)[:, None] * freqs[None, :]
    cosine = jnp.concatenate([jnp.cos(angles)] * 2, axis=1)
    sine = jnp.concatenate([-jnp.sin(angles), jnp.sin(angles)], axis=1)
    index = jnp.arange(block, dtype=jnp.int32)
    visible = (index[None, :] <= index[:, None]) & (index[None, :] >= (index - spots)[:, None])
    nq = query_new.shape[2]
    mask = jnp.concatenate([visible.astype(F32)] * (nq // HEAD_SIZE), axis=0)

    start = jnp.stack(
        [
            lax.dynamic_index_in_dim(inputs, pipe, 0, keepdims=False),
            lax.dynamic_index_in_dim(out_grads, pipe, 0, keepdims=False),
        ]
    )
    start = start.reshape(2, own, n_dp, feats).transpose(2, 0, 1, 3).reshape(n_dp * 2 * own, feats)
    start = dp_exchange(start).reshape(n_dp, 2, own, feats)
    h0 = start[:, 0].reshape(n_dp * own, feats)
    g1 = start[:, 1].reshape(n_dp * own, feats)

    def gather_z(tiled):
        mine = z_exchange(tiled)
        return mine, swap(mine, "tensor", 1)

    def scatter_z(part_mine, part_other):
        moved = swap(part_other, "tensor", 1)
        return z_exchange((part_mine + moved.astype(F32)).astype(BF))

    def head_rows(columns):
        return [((n_dp * block, columns), BF)]

    sent_columns = nq + 2 * HEAD_SIZE + 128

    h0_mine, h0_other = gather_z(tile_rows(h0, nz))
    part = project(target, h0_mine, h0_other, wq0, wkv0)
    part, g1_sent, own_out, kv_next = lax.optimization_barrier((part, g1, out_new[0], kv_next))
    got = dp_exchange(part)
    all_g1 = lax.all_gather(g1_sent, "tensor", axis=0, tiled=True)
    wo0, wo1 = arrange(own_out, swap(own_out, "pipe", 1))
    wkv1 = whole_head(kv_next)
    mixed0, total0 = call(
        functools.partial(forward_body, nq, width),
        head_rows(nq) + [((block, sent_columns), F32)],
        got,
        cosine,
        sine,
        mask,
    )
    got_m0, all_g1 = lax.optimization_barrier((dp_exchange(mixed0), all_g1))
    all_m0, far0, near0 = out_project(target, got_m0, wo0)
    h1, h1_tiled = settle(scatter_z(near0, far0), h0)

    dm1 = mixed_grad(by_rank, [all_g1], wo1)
    h1_mine, h1_other = gather_z(h1_tiled)
    got = dp_exchange(project(target, h1_mine, h1_other, wq1, wkv1, dm1))
    sent1 = call(
        functools.partial(both_body, nq, width),
        head_rows(sent_columns + nq),
        got,
        cosine,
        sine,
        mask,
    )[0]
    got1 = dp_exchange(sent1)
    rows1, far1, near1 = back_project(target, got1, h1_mine, h1_other, wq1, wkv1)
    g0, g0_tiled = settle(scatter_z(near1, far1), g1)

    def section_grads(rows, mine, other):
        grad_q = mm(mine, rows[:half, :nq], 0, 0) + mm(other, rows[half:, :nq], 0, 0)
        grad_kv = mm(rows[:half, nq:], mine, 0, 0) + mm(rows[half:, nq:], other, 0, 0)
        return grad_q, grad_kv

    g0_mine, g0_other = gather_z(g0_tiled)
    gq1, gkv1 = section_grads(rows1, h1_mine, h1_other)
    all_m1, term1 = whole_project(by_rank, got1[:, sent_columns:], wo1)
    go1 = mm(all_m1, all_g1, 0, 0)
    out1 = lax.psum_scatter(term1, "tensor", scatter_dimension=0, tiled=True)
    h2 = (h1.astype(F32) + out1.astype(F32)).astype(BF)
    got_dm0 = dp_exchange(mixed_grad(target, [g0_mine, g0_other], wo0))
    sent0 = call(
        functools.partial(backward_body, nq, width),
        head_rows(sent_columns),
        total0,
        got_dm0,
        cosine,
        sine,
        mask,
    )[0]
    go0 = mm(all_m0[:half], g0_mine, 0, 0) + mm(all_m0[half:], g0_other, 0, 0)
    rows0, far, near = back_project(target, dp_exchange(sent0), h0_mine, h0_other, wq0, wkv0)
    gi, _ = settle(scatter_z(near, far), g0)
    gq0, gkv0 = section_grads(rows0, h0_mine, h0_other)

    def kv_columns(grad):
        cols = grad.shape[0] // 4
        quarters = grad.astype(BF).reshape(2, 2, cols, feats)
        keep = lax.dynamic_index_in_dim(quarters, core, 1, keepdims=False)
        send = lax.dynamic_index_in_dim(quarters, 1 - core, 1, keepdims=False)
        pair = keep.astype(F32) + swap(send, "tensor", 1).astype(F32)
        pair = pair.astype(BF)
        zz = (rank // 2) % 2
        keep = lax.dynamic_index_in_dim(pair, zz, 0, keepdims=False)
        send = lax.dynamic_index_in_dim(pair, 1 - zz, 0, keepdims=False)
        return keep.astype(F32) + swap(send, "tensor", 2).astype(F32)

    def home(grad0, grad1):
        to1 = lax.ppermute(grad1.astype(BF), "pipe", [(0, 1)])
        to0 = lax.ppermute(grad0.astype(BF), "pipe", [(1, 0)])
        return jnp.where(first, grad0 + to0.astype(F32), grad1 + to1.astype(F32))

    query_grad = home(gq0, gq1)
    kv_grad = home(kv_columns(gkv0), kv_columns(gkv1)).T
    out_grad = home(go0, go1)

    ends = jnp.stack([h1, gi, h2, g0]).reshape(2, 2, n_dp, own, feats).transpose(2, 0, 1, 3, 4)
    ends = lax.all_to_all(
        ends.reshape(n_dp * 4 * own, feats), ("dp", "pipe"), 0, 0, tiled=True
    ).reshape(n_dp, micro, 2, own, feats)
    rows = ends.transpose(2, 1, 3, 0, 4).reshape(2, micro, own, width)
    return (
        rows[0][None],
        rows[1][None],
        query_new,
        kv_new,
        out_new,
        query_grad[None],
        kv_grad[None],
        out_grad[None],
    )


def solution(mesh):
    placed = (
        P(None, ("dp", "tensor"), None),
        P(None, "dp"),
        P(None, ("dp", "tensor"), None),
        P("pipe", "dp", "tensor"),
        P("pipe", "dp", "tensor"),
        P("pipe", "tensor", "dp"),
        P("pipe", "dp", "tensor"),
        P("pipe", "dp", "tensor"),
        P("pipe", "tensor", "dp"),
    )
    return jax.shard_map(
        shards,
        mesh=mesh,
        in_specs=placed,
        out_specs=(
            P("pipe", None, ("dp", "tensor"), None),
            P("pipe", None, ("dp", "tensor"), None),
            P("pipe", "dp", "tensor"),
            P("pipe", "dp", "tensor"),
            P("pipe", "tensor", "dp"),
            P("pipe", "dp", "tensor"),
            P("pipe", "dp", "tensor"),
            P("pipe", "tensor", "dp"),
        ),
        check_vma=False,
    )
```

```python
import functools
import math

import jax
import jax.numpy as jnp
from jax import lax
from jax.experimental import pallas as pl
from jax.experimental.pallas import tpu as pltpu
from jax.sharding import PartitionSpec as P

HEAD_SIZE = 128
EPS = 1e-05
THETA = 500000.0
LR = 0.5
BF = jnp.bfloat16
F32 = jnp.float32


def mm(a, b, ca=1, cb=0):
    return lax.dot_general(a, b, (((ca,), (cb,)), ((), ())), preferred_element_type=F32)


def swap(value, axis, mask):
    pairs = [(source, source ^ mask) for source in range(lax.axis_size(axis))]
    return lax.ppermute(value, axis, pairs)


def exchange(value, groups):
    return lax.all_to_all(value, "tensor", 0, 0, axis_index_groups=groups, tiled=True)


def dp_exchange(value):
    return lax.all_to_all(value, "dp", 0, 0, tiled=True)


def tile_rows(value, copies):
    return jnp.broadcast_to(value[None], (copies,) + value.shape).reshape(
        (copies * value.shape[0],) + value.shape[1:]
    )


def call(body, shapes, *operands, flops=0, deps=()):
    outs, specs, kept, sent = [], [], [], []
    for i, (shape, kind, copies) in enumerate(shapes):
        if copies:
            outs.append(jax.ShapeDtypeStruct((copies * shape[0], shape[1]), kind))
            specs.append(pl.BlockSpec(memory_space=pltpu.HBM))
            kept.append(pltpu.VMEM(shape, kind))
            sent.append((i, copies))
        else:
            outs.append(jax.ShapeDtypeStruct(shape, kind))
            specs.append(pl.BlockSpec(shape, lambda i: (0, 0)))
    count = sum(copies for _, copies in sent)
    first = len(operands)
    extra = len(deps)

    def plain(*refs):
        body(*refs[:first], *refs[first + extra :])

    def whole(*refs):
        refs = refs[:first] + refs[first + extra :]
        ends = list(refs[first : first + len(outs)])
        buffers = refs[first + len(outs) :]
        finals = []
        for (i, copies), buffer in zip(sent, buffers):
            finals.append((ends[i], copies, buffer))
            ends[i] = buffer
        body(*refs[:first], *ends)
        moves = []
        for final, copies, buffer in finals:
            rows = buffer.shape[0]
            for k in range(copies):
                where = final.at[pl.ds(k * rows, rows)]
                move = pltpu.make_async_copy(buffer, where, buffers[-1].at[len(moves)])
                move.start()
                moves.append(move)
        for move in moves:
            move.wait()

    moved = sum(x.size * x.dtype.itemsize for x in list(operands) + outs)
    return pl.pallas_call(
        whole if sent else plain,
        out_shape=outs,
        grid=(1,),
        in_specs=[pl.BlockSpec(memory_space=pltpu.VMEM)] * first
        + [pl.BlockSpec(memory_space=pl.ANY)] * extra,
        out_specs=specs,
        scratch_shapes=kept + ([pltpu.SemaphoreType.DMA((count,))] if sent else []),
        compiler_params=pltpu.CompilerParams(vmem_limit_bytes=20 * 2**20),
        cost_estimate=pl.CostEstimate(flops=flops, bytes_accessed=moved, transcendentals=0),
    )(*operands, *deps)


def nothing(*refs):
    pass


def tie(value, *others):
    return pl.pallas_call(
        nothing,
        out_shape=jax.ShapeDtypeStruct(value.shape, value.dtype),
        in_specs=[pl.BlockSpec(memory_space=pl.ANY)] * (1 + len(others)),
        out_specs=pl.BlockSpec(memory_space=pl.ANY),
        input_output_aliases={0: 0},
    )(value, *others)


def one_hot(target):
    size = target.shape[1]
    row = lax.broadcasted_iota(jnp.int32, (size, size), 0)
    return jnp.where(row == target, 1.0, 0.0).astype(BF)


def pair_columns(column):
    high = column.astype(BF).astype(F32)
    lane = lax.broadcasted_iota(jnp.int32, (column.shape[0], 128), 1)
    return jnp.where(lane == 0, high, jnp.where(lane == 1, column - high, 0.0)).astype(BF)


def project_body(tokens, target, mine, other, wq, wkv, *rest):
    half = mine.shape[0]
    nq = wq.shape[1]
    parts = []
    for rows in (mine[...], other[...]):
        wide = rows.astype(F32)
        squares = jnp.sum(wide * wide, axis=1, keepdims=True)
        parts.append(
            jnp.concatenate(
                [mm(rows, wq[...]).astype(BF), mm(rows, wkv[...], 1, 1).astype(BF), pair_columns(squares)],
                axis=1,
            )
        )
    order = one_hot(target[...])
    value = (mm(order[:, :half], parts[0]) + mm(order[:, half:], parts[1])).astype(BF)
    out = rest[-1]
    lot = nq // 2
    for k in range(out.shape[0] // tokens):
        rows = slice((k // 2) * tokens, (k // 2 + 1) * tokens)
        cols = slice((k % 2) * lot, (k % 2 + 1) * lot)
        pieces = [value[rows, cols], value[rows, nq:]]
        if len(rest) > 1:
            pieces.append(rest[0][rows, cols])
        out[k * tokens : (k + 1) * tokens] = jnp.concatenate(pieces, axis=1)


def project(tokens, target, mine, other, wq, wkv, *extra):
    rows = 2 * mine.shape[0]
    cols = wq.shape[1] + wkv.shape[0] + 128
    flops = 2 * rows * cols * (mine.shape[1] + rows)
    cols = cols - wq.shape[1] // 2 + sum(x.shape[1] // 2 for x in extra)
    return call(
        functools.partial(project_body, tokens),
        [((2 * rows, cols), BF, 1)],
        target,
        mine,
        other,
        wq,
        wkv,
        *extra,
        flops=flops,
    )[0]


def mixed_grad_body(tokens, target, mine, other, wo, out):
    half = mine.shape[0]
    parts = [mm(x[...], wo[...], 1, 1).astype(BF) for x in (mine, other)]
    order = one_hot(target[...])
    value = (mm(order[:, :half], parts[0]) + mm(order[:, half:], parts[1])).astype(BF)
    if tokens is None:
        out[...] = value
        return
    lot = value.shape[1] // 2
    for k in range(out.shape[0] // tokens):
        rows = slice((k // 2) * tokens, (k // 2 + 1) * tokens)
        out[k * tokens : (k + 1) * tokens] = value[rows, (k % 2) * lot : (k % 2 + 1) * lot]


def mixed_grad(tokens, target, mine, other, wo):
    rows = target.shape[1]
    cols = wo.shape[0]
    flops = 2 * rows * cols * (wo.shape[1] + rows)
    shape = (rows, cols) if tokens is None else (2 * rows, cols // 2)
    body = functools.partial(mixed_grad_body, tokens)
    copies = 0 if tokens is None else 1
    return call(body, [(shape, BF, copies)], target, mine, other, wo, flops=flops)[0]


def side_by_side(got, tokens, lo, hi):
    pairs = []
    for k in range(0, got.shape[0] // tokens, 2):
        left = got[k * tokens : (k + 1) * tokens, lo:hi]
        right = got[(k + 1) * tokens : (k + 2) * tokens, lo:hi]
        pairs.append(jnp.concatenate([left, right], axis=1))
    return jnp.concatenate(pairs, axis=0)


def summed(got, tokens, lo, hi):
    pairs = []
    for k in range(0, got.shape[0] // tokens, 2):
        left = got[k * tokens : (k + 1) * tokens, lo:hi].astype(F32)
        pairs.append(left + got[(k + 1) * tokens : (k + 2) * tokens, lo:hi].astype(F32))
    return jnp.concatenate(pairs, axis=0)


def out_body(tokens, target, got, wo, rows_out, other_out, mine_out):
    half = mine_out.shape[0]
    held = side_by_side(got, tokens, 0, got.shape[1])
    rows = mm(one_hot(target[...]), held, 0, 0).astype(BF)
    rows_out[...] = rows
    other_out[...] = mm(rows[half:], wo[...]).astype(BF)
    mine_out[...] = mm(rows[:half], wo[...])


def out_project(tokens, target, got, wo, *deps):
    rows, cols = got.shape[0] // 2, got.shape[1] * 2
    feats = wo.shape[1]
    return call(
        functools.partial(out_body, tokens),
        [((rows, cols), BF, 0), ((rows // 2, feats), BF, 0), ((rows // 2, feats), F32, 0)],
        target,
        got,
        wo,
        flops=2 * rows * cols * (rows + feats),
        deps=deps,
    )


def back_body(tokens, target, got, mine, other, wq, wkv, rows_out, other_out, mine_out):
    half = mine.shape[0]
    nq = wq.shape[1]
    lot = nq // 2
    end = lot + wkv.shape[0]
    coef = jnp.sum(summed(got, tokens, end, end + 128), axis=1, keepdims=True)
    held = jnp.concatenate(
        [
            side_by_side(got, tokens, 0, lot),
            summed(got, tokens, lot, end).astype(BF),
            pair_columns(coef),
        ],
        axis=1,
    )
    rows = mm(one_hot(target[...]), held, 0, 0)
    end = nq + wkv.shape[0]
    coef = jnp.sum(rows[:, end:], axis=1, keepdims=True)
    low = rows[:, :end].astype(BF)
    rows_out[...] = low

    def term(part, c, kept):
        value = mm(part[:, :nq], wq[...], 1, 1) + mm(part[:, nq:], wkv[...])
        return value - kept[...].astype(F32) * c

    other_out[...] = term(low[half:], coef[half:], other).astype(BF)
    mine_out[...] = term(low[:half], coef[:half], mine)


def back_project(tokens, target, got, mine, other, wq, wkv):
    rows = 2 * mine.shape[0]
    cols = wq.shape[1] + wkv.shape[0]
    feats = mine.shape[1]
    return call(
        functools.partial(back_body, tokens),
        [((rows, cols), BF, 0), ((rows // 2, feats), BF, 0), ((rows // 2, feats), F32, 0)],
        target,
        got,
        mine,
        other,
        wq,
        wkv,
        flops=2 * rows * (cols + 128) * (rows + feats),
    )


def settle_body(count, got, held, *outs):
    rows = held.shape[0]
    total = held[...].astype(F32)
    for i in range(count):
        total = total + got[i * rows : (i + 1) * rows].astype(F32)
    low = total.astype(BF)
    for out in outs:
        out[...] = low


def settle(got, held, *copies):
    count = got.shape[0] // held.shape[0]
    return call(
        functools.partial(settle_body, count),
        [(held.shape, BF, k) for k in copies],
        got,
        held,
    )


def copy_body(value, out):
    out[...] = value[...]


def turn(value, cosine, sine):
    return value * cosine + pltpu.roll(value, HEAD_SIZE // 2, 1) * sine


def heads_down(value):
    count = value.shape[1] // HEAD_SIZE
    return jnp.concatenate(
        [value[:, i * HEAD_SIZE : (i + 1) * HEAD_SIZE] for i in range(count)], axis=0
    )


def heads_across(value, tokens):
    count = value.shape[0] // tokens
    return jnp.concatenate([value[i * tokens : (i + 1) * tokens] for i in range(count)], axis=1)


def add_parts(ref, tokens):
    total = ref[:tokens].astype(F32)
    for i in range(1, ref.shape[0] // tokens):
        total = total + ref[i * tokens : (i + 1) * tokens].astype(F32)
    return total


def look(total, nq, width, cosine, sine, mask):
    tokens = total.shape[0]
    heads = nq // HEAD_SIZE
    end = nq + 2 * HEAD_SIZE
    squares = jnp.sum(total[:, end:], axis=1, keepdims=True)
    scale = lax.rsqrt(squares / width + EPS)
    wide_cos = jnp.concatenate([cosine] * heads, axis=0)
    wide_sin = jnp.concatenate([sine] * heads, axis=0)
    queries = turn(heads_down(total[:, :nq] * scale), wide_cos, wide_sin).astype(BF)
    kv = (total[:, nq:end] * scale).astype(BF)
    keys = turn(kv[:, :HEAD_SIZE].astype(F32), cosine, sine).astype(BF)
    values = kv[:, HEAD_SIZE:]
    scores = mm(queries, keys, 1, 1) * (1.0 / math.sqrt(HEAD_SIZE))
    weights = jnp.exp(jnp.where(mask > 0.0, scores, -1e30))
    probs = weights / jnp.sum(weights, axis=1, keepdims=True)
    low = probs.astype(BF)
    return scale, queries, keys, values, probs, low, wide_cos, wide_sin


def look_back(total, d_mixed, nq, width, cosine, sine, seen):
    scale, queries, keys, values, probs, low, wide_cos, wide_sin = seen
    tokens = total.shape[0]
    end = nq + 2 * HEAD_SIZE
    dm = heads_down(d_mixed).astype(BF)
    d_probs = mm(dm, values, 1, 1)
    d_values = mm(low, dm, 0, 0)
    d_scores = probs * (d_probs - jnp.sum(probs * d_probs, axis=1, keepdims=True))
    d_scores = (d_scores * (1.0 / math.sqrt(HEAD_SIZE))).astype(BF)
    dq = turn(mm(d_scores, keys), wide_cos, -wide_sin)
    dk = turn(mm(d_scores, queries, 0, 0), cosine, -sine)
    dq = (heads_across(dq, tokens) * scale).astype(BF)
    dkv = (jnp.concatenate([dk, d_values], axis=1) * scale).astype(BF)
    both = jnp.concatenate([dq, dkv], axis=1)
    dot = jnp.sum(both.astype(F32) * total[:, :end], axis=1, keepdims=True)
    return jnp.concatenate([both, pair_columns(dot * scale * scale / width)], axis=1)


def forward_body(nq, width, got, cosine, sine, mask, mixed_out, total_out):
    tokens = cosine.shape[0]
    total = add_parts(got, tokens)
    total_out[...] = total
    seen = look(total, nq, width, cosine[...], sine[...], mask[...])
    mixed_out[...] = heads_across(mm(seen[5], seen[3]), tokens).astype(BF)


def both_body(nq, width, got, cosine, sine, mask, sent_out):
    tokens = cosine.shape[0]
    total = add_parts(got, tokens)
    d_mixed = total[:, total.shape[1] - nq :]
    total = total[:, : total.shape[1] - nq]
    seen = look(total, nq, width, cosine[...], sine[...], mask[...])
    mixed = heads_across(mm(seen[5], seen[3]), tokens).astype(BF)
    sent = look_back(total, d_mixed, nq, width, cosine[...], sine[...], seen)
    sent_out[...] = jnp.concatenate([sent, mixed], axis=1)


def backward_body(nq, width, total, grads, cosine, sine, mask, sent_out):
    tokens = cosine.shape[0]
    d_mixed = add_parts(grads, tokens)
    seen = look(total[...], nq, width, cosine[...], sine[...], mask[...])
    sent_out[...] = look_back(total[...], d_mixed, nq, width, cosine[...], sine[...], seen)


def shards(
    inputs,
    positions,
    out_grads,
    query_weight,
    key_value_weight,
    out_weight,
    query_stale,
    key_value_previous_gradient,
    out_stale,
):
    n_dp = lax.axis_size("dp")
    ranks = lax.axis_size("tensor")
    pipe = lax.axis_index("pipe")
    rank = lax.axis_index("tensor")
    core = rank % 2
    odd = (rank // 2) % 2
    far_pair = rank // 4
    first = pipe == 0
    even = odd == 0
    micro, own, width = inputs.shape
    feats = width // n_dp
    block = own * ranks
    some = n_dp // 2
    tokens = some * block
    half = tokens // 2
    slab = n_dp * own
    chips = [list(range(c, ranks, 2)) for c in range(2)]
    alike = [list(range(c, ranks, 4)) for c in range(4)]

    query_new = (query_weight.astype(F32) - LR * query_stale).astype(BF)
    kv_new = (key_value_weight.astype(F32) - LR * key_value_previous_gradient).astype(BF)
    out_new = (out_weight.astype(F32) - LR * out_stale).astype(BF)

    def after(value, *others):
        return lax.optimization_barrier((value,) + others)[0]

    def arrange(own_part):
        other = swap(own_part, "pipe", 1)
        return jnp.where(first, own_part, other), jnp.where(first, other, own_part)

    def in_order(flag, own_part, other, axis):
        return jnp.where(
            flag,
            jnp.concatenate([own_part, other], axis=axis),
            jnp.concatenate([other, own_part], axis=axis),
        )

    def of_pair(own_part, other, axis):
        return in_order(even, own_part, other, axis)

    def head_half(own_part):
        return in_order(core == 0, own_part, swap(own_part, "tensor", 1), 0)

    def with_far(own_part, axis):
        return of_pair(own_part, swap(own_part, "tensor", 2), axis)

    far_q = swap(query_new[0], "tensor", 2)
    kv_here, kv_next = arrange(kv_new[0].T)
    pair0 = head_half(kv_here)

    at = lax.broadcasted_iota(jnp.int32, (1, tokens), 1)
    inside = at % half
    chip = inside // (some * own)
    rest = inside % (some * own)
    target = (rest // own) * block + (chip * 2 + ((at // half) ^ core)) * own + rest % own

    size = lax.axis_size("pipe")

    def source(d, p, r):
        b = some * ((r // 2) % 2) + d // 2
        return (b * size + p) * ranks + (2 * (r // 4) + d % 2) * 2 + r % 2

    spots = lax.ppermute(
        positions,
        ("dp", "pipe", "tensor"),
        [
            (source(d, p, r), (d * size + p) * ranks + r)
            for d in range(n_dp)
            for p in range(size)
            for r in range(ranks)
        ],
    )
    spots = lax.dynamic_index_in_dim(spots, pipe, 0, keepdims=False)
    freqs = THETA ** (-2.0 * jnp.arange(HEAD_SIZE // 2, dtype=F32) / HEAD_SIZE)
    angles = spots.astype(F32)[:, None] * freqs[None, :]
    cosine = jnp.concatenate([jnp.cos(angles)] * 2, axis=1)
    sine = jnp.concatenate([-jnp.sin(angles), jnp.sin(angles)], axis=1)
    index = jnp.arange(block, dtype=jnp.int32)
    visible = (index[None, :] <= index[:, None]) & (index[None, :] >= (index - spots)[:, None])
    nq = query_new.shape[2]
    mask = jnp.concatenate([visible.astype(F32)] * (nq // HEAD_SIZE), axis=0)

    start = jnp.stack(
        [
            lax.dynamic_index_in_dim(inputs, pipe, 0, keepdims=False),
            lax.dynamic_index_in_dim(out_grads, pipe, 0, keepdims=False),
        ]
    )
    start = start.reshape(2, own, n_dp, feats).transpose(2, 0, 1, 3).reshape(2 * slab, feats)
    start = dp_exchange(start)
    wkv0 = with_far(pair0, 0)
    start = start.reshape(2, some, 2, own, feats).transpose(0, 2, 1, 3, 4)
    start = start.reshape(2 * slab, feats)

    def gather_z(tiled):
        mine = exchange(tiled, alike)
        return mine, swap(mine, "tensor", 1)

    def add_pair(part_mine, part_other):
        moved = swap(part_other, "tensor", 1)
        return (part_mine + moved.astype(F32)).astype(BF)

    def head_rows(columns):
        return [((block, columns), BF, n_dp)]

    sent_columns = nq + 2 * HEAD_SIZE + 128
    near_chips = ranks // 4

    begin = call(copy_body, [(start.shape, BF, near_chips)], start, deps=[wkv0])[0]
    wq0, wq1 = arrange(of_pair(query_new[0], tie(far_q, begin), 1))
    begin = exchange(begin, chips)
    begin = begin.reshape(ranks // 2, 2, some * own, feats)
    h0_mine = after(begin[:, 0].reshape(half, feats), wq0, wkv0, wq1, out_new)
    g1_mine = begin[:, 1].reshape(half, feats)
    h0_other = swap(h0_mine, "tensor", 1)
    part = project(block, target, h0_mine, h0_other, wq0, wkv0)
    g1_sent = after(g1_mine, part)
    g1_other = swap(g1_sent, "tensor", 1)
    out_here, out_next = arrange(after(out_new[0], wq0))
    got = dp_exchange(part)
    wo0 = with_far(after(out_here, part), 0)
    wkv1 = with_far(after(head_half(kv_next), part), 0)
    h0 = lax.dynamic_slice_in_dim(h0_mine, far_pair * slab, slab, 0)
    g1 = lax.dynamic_slice_in_dim(g1_mine, far_pair * slab, slab, 0)
    mixed0, total0 = call(
        functools.partial(forward_body, nq, width),
        head_rows(nq) + [((block, sent_columns), F32, 1)],
        got,
        cosine,
        sine,
        mask,
    )
    all_m0, far0, near0 = out_project(block, target, dp_exchange(mixed0), wo0, wkv1)
    wo1 = of_pair(out_next, swap(tie(out_next, mixed0), "tensor", 2), 0)
    reduced = exchange(add_pair(near0, far0), alike)
    h1, h1_tiled = settle(after(reduced, g1_other), h0, 0, near_chips)

    dm1 = mixed_grad(None, target, g1_mine, g1_other, wo1)
    h1_mine = after(exchange(h1_tiled, alike), dm1)
    h1_other = swap(h1_mine, "tensor", 1)
    got = dp_exchange(project(block, target, h1_mine, h1_other, wq1, wkv1, dm1))
    sent1 = call(
        functools.partial(both_body, nq, width),
        head_rows(sent_columns + nq),
        got,
        cosine,
        sine,
        mask,
    )[0]
    got1 = dp_exchange(sent1)
    rows1, far1, near1 = back_project(block, target, got1, h1_mine, h1_other, wq1, wkv1)
    sent_back = add_pair(near1, far1)
    rows1 = tie(rows1, sent_back)
    g0, g0_tiled = settle(exchange(sent_back, alike), g1, 0, near_chips)

    def halves(rows):
        cut = [rows[:, :nq], rows[:, nq : 2 * nq]]
        return jnp.where(even, cut[0], cut[1]), jnp.where(even, cut[1], cut[0])

    def grads_q(rows, mine, other):
        return [
            mm(mine, x[:half], 0, 0) + mm(other, x[half:], 0, 0) for x in halves(rows[:, : 2 * nq])
        ]

    def grads_o(rows, mine, other):
        return [mm(x[:half], mine, 0, 0) + mm(x[half:], other, 0, 0) for x in halves(rows)]

    def grads_kv(rows, mine, other):
        low = rows[:, 2 * nq :]
        return mm(low[:half], mine, 0, 0) + mm(low[half:], other, 0, 0)

    def with_partner(own_grad, partner_grad, early, late):
        moved = swap(tie(partner_grad.astype(BF), early), "tensor", 2)
        return own_grad + tie(moved, late).astype(F32)

    gq1 = grads_q(rows1, h1_mine, h1_other)
    gkv1 = grads_kv(rows1, h1_mine, h1_other)
    all_m1, far_o, near_o = out_project(block, target, got1[:, sent_columns:], wo1, sent_back)
    pair1 = add_pair(near_o, far_o)
    go1 = grads_o(all_m1, g1_mine, g1_other)
    g0_mine = after(exchange(g0_tiled, alike), *gq1, *go1, gkv1, pair1)
    g0_other = swap(g0_mine, "tensor", 1)
    dm0 = mixed_grad(block, target, g0_mine, g0_other, wo0)
    gkv1 = after(gkv1, dm0)
    got_dm0 = dp_exchange(dm0)
    sent0 = call(
        functools.partial(backward_body, nq, width),
        head_rows(sent_columns),
        total0,
        got_dm0,
        cosine,
        sine,
        mask,
    )[0]
    go0 = grads_o(after(all_m0, dm0), g0_mine, g0_other)

    def at_home(rows):
        parts = rows.reshape(2, -1, feats)
        keep = lax.dynamic_index_in_dim(parts, odd, 0, keepdims=False)
        send = lax.dynamic_index_in_dim(parts, 1 - odd, 0, keepdims=False)
        return in_order(even, keep, swap(send, "tensor", 2), 0)

    h1_home, g0_home = at_home(after(h1, dm0)), at_home(after(g0, dm0))
    rows0, far, near = back_project(
        block, target, dp_exchange(sent0), h0_mine, h0_other, wq0, wkv0
    )
    both = [x.reshape(ranks // 2, -1, feats) for x in (add_pair(near, far), pair1)]
    both = jnp.concatenate(both, axis=1).reshape(2 * half, feats)
    rows0 = tie(rows0, both)
    gq0 = grads_q(rows0, h0_mine, h0_other)
    gkv0 = grads_kv(rows0, h0_mine, h0_other)
    last = exchange(both, chips)
    held = [x.reshape(2, -1, feats) for x in (g0_home, h1_home)]
    ends = settle(last, jnp.concatenate(held, axis=1).reshape(2 * slab, feats), 0)[0]
    ends = ends.reshape(2, 2, some * own, feats)
    gi, h2 = ends[:, 0].reshape(slab, feats), ends[:, 1].reshape(slab, feats)

    def home(grad0, grad1, *late):
        to1 = lax.ppermute(grad1.astype(BF), "pipe", [(0, 1)])
        to0 = lax.ppermute(grad0.astype(BF), "pipe", [(1, 0)])
        to0 = tie(to0, *late) if late else to0
        return jnp.where(first, grad0 + to0.astype(F32), grad1 + to1.astype(F32))

    def kv_sums(grad, early):
        quarters = grad.astype(BF).reshape(2, 2, grad.shape[0] // 4, feats)
        keep = lax.dynamic_index_in_dim(quarters, core, 1, keepdims=False)
        send = lax.dynamic_index_in_dim(quarters, 1 - core, 1, keepdims=False)
        return keep.astype(F32) + swap(after(send, early), "tensor", 1).astype(F32)

    sums = [
        with_partner(*gq1, dm0, sent0),
        with_partner(*go1, dm0, sent0),
        with_partner(*go0, sent0, both),
        with_partner(*gq0, both, last),
    ]
    query_grad = home(sums[3], sums[0])
    out_grad = home(sums[2], sums[1])
    kv_pair = home(kv_sums(gkv0, both), kv_sums(gkv1, got_dm0), sums[3]).astype(BF)
    keep = lax.dynamic_index_in_dim(kv_pair, odd, 0, keepdims=False)
    send = lax.dynamic_index_in_dim(kv_pair, 1 - odd, 0, keepdims=False)
    kv_grad = (keep.astype(F32) + swap(after(send, last), "tensor", 2).astype(F32)).T

    ends = jnp.stack([h1_home, gi, h2, g0_home])
    ends = ends.reshape(2, 2, n_dp, own, feats).transpose(2, 0, 1, 3, 4)
    ends = lax.all_to_all(
        ends.reshape(n_dp * 4 * own, feats), ("dp", "pipe"), 0, 0, tiled=True
    ).reshape(n_dp, micro, 2, own, feats)
    rows = ends.transpose(2, 1, 3, 0, 4).reshape(2, micro, own, width)
    return (
        rows[0][None],
        rows[1][None],
        query_new,
        kv_new,
        out_new,
        query_grad[None],
        kv_grad[None],
        out_grad[None],
    )


def solution(mesh):
    placed = (
        P(None, ("dp", "tensor"), None),
        P(None, "dp"),
        P(None, ("dp", "tensor"), None),
        P("pipe", "dp", "tensor"),
        P("pipe", "dp", "tensor"),
        P("pipe", "tensor", "dp"),
        P("pipe", "dp", "tensor"),
        P("pipe", "dp", "tensor"),
        P("pipe", "tensor", "dp"),
    )
    return jax.shard_map(
        shards,
        mesh=mesh,
        in_specs=placed,
        out_specs=(
            P("pipe", None, ("dp", "tensor"), None),
            P("pipe", None, ("dp", "tensor"), None),
            P("pipe", "dp", "tensor"),
            P("pipe", "dp", "tensor"),
            P("pipe", "tensor", "dp"),
            P("pipe", "dp", "tensor"),
            P("pipe", "dp", "tensor"),
            P("pipe", "tensor", "dp"),
        ),
        check_vma=False,
    )
```

```python
import functools
import math

import jax
import jax.numpy as jnp
from jax import lax
from jax.experimental import pallas as pl
from jax.experimental.pallas import tpu as pltpu
from jax.sharding import PartitionSpec as P

HEAD_SIZE = 128
EPS = 1e-05
THETA = 500000.0
LR = 0.5
BF = jnp.bfloat16
F32 = jnp.float32


def mm(a, b, ca=1, cb=0):
    return lax.dot_general(a, b, (((ca,), (cb,)), ((), ())), preferred_element_type=F32)


def swap(value, axis, mask):
    pairs = [(source, source ^ mask) for source in range(lax.axis_size(axis))]
    return lax.ppermute(value, axis, pairs)


def same_core(size):
    return [list(range(c, size, 2)) for c in range(2)]


def z_exchange(value):
    size = lax.axis_size("tensor")
    return lax.all_to_all(
        value, "tensor", 0, 0, axis_index_groups=same_core(size), tiled=True
    )


def dp_exchange(value):
    return lax.all_to_all(value, "dp", 0, 0, tiled=True)


def tile_rows(value, copies):
    return jnp.broadcast_to(value[None], (copies,) + value.shape).reshape(
        (copies * value.shape[0],) + value.shape[1:]
    )


def call(body, shapes, *operands, flops=0, deps=()):
    first, extra = len(operands), len(deps)

    def plain(*refs):
        body(*refs[:first], *refs[first + extra :])

    outs = [jax.ShapeDtypeStruct(shape, kind) for shape, kind in shapes]
    moved = sum(x.size * x.dtype.itemsize for x in list(operands) + outs)
    return pl.pallas_call(
        plain,
        out_shape=outs,
        in_specs=[pl.BlockSpec(memory_space=pltpu.VMEM)] * first
        + [pl.BlockSpec(memory_space=pl.ANY)] * extra,
        out_specs=[pl.BlockSpec(memory_space=pltpu.VMEM)] * len(outs),
        compiler_params=pltpu.CompilerParams(vmem_limit_bytes=48 * 2**20),
        cost_estimate=pl.CostEstimate(flops=flops, bytes_accessed=moved, transcendentals=0),
    )(*operands, *deps)


def one_hot(target):
    size = target.shape[1]
    row = lax.broadcasted_iota(jnp.int32, (size, size), 0)
    return jnp.where(row == target, 1.0, 0.0).astype(BF)


def pair_columns(column):
    high = column.astype(BF).astype(F32)
    lane = lax.broadcasted_iota(jnp.int32, (column.shape[0], 128), 1)
    return jnp.where(lane == 0, high, jnp.where(lane == 1, column - high, 0.0)).astype(BF)


def project_body(target, mine, other, wq, wkv, *rest):
    half = mine.shape[0]
    parts = []
    for rows in (mine[...], other[...]):
        wide = rows.astype(F32)
        squares = jnp.sum(wide * wide, axis=1, keepdims=True)
        parts.append(
            jnp.concatenate(
                [mm(rows, wq[...]).astype(BF), mm(rows, wkv[...], 1, 1).astype(BF), pair_columns(squares)],
                axis=1,
            )
        )
    order = one_hot(target[...])
    value = (mm(order[:, :half], parts[0]) + mm(order[:, half:], parts[1])).astype(BF)
    out = rest[-1]
    out[:, : value.shape[1]] = value
    if len(rest) > 1:
        out[:, value.shape[1] :] = rest[0][...]


def project(target, mine, other, wq, wkv, *extra):
    rows = 2 * mine.shape[0]
    cols = wq.shape[1] + wkv.shape[0] + 128
    flops = 2 * rows * cols * (mine.shape[1] + rows)
    cols = cols + sum(x.shape[1] for x in extra)
    return call(
        project_body, [((rows, cols), BF)], target, mine, other, wq, wkv, *extra, flops=flops
    )[0]


def mixed_grad_body(target, *refs):
    wo, out = refs[-2:]
    order = one_hot(target[...])
    total = None
    at = 0
    for part in refs[:-2]:
        count = part.shape[0]
        low = mm(part[...], wo[...], 1, 1).astype(BF)
        value = mm(order[:, at : at + count], low)
        total = value if total is None else total + value
        at = at + count
    out[...] = total.astype(BF)


def mixed_grad(target, parts, wo):
    rows = target.shape[1]
    cols = wo.shape[0]
    flops = 2 * rows * cols * (wo.shape[1] + rows)
    return call(mixed_grad_body, [((rows, cols), BF)], target, *parts, wo, flops=flops)[0]


def whole_body(target, got, wo, rows_out, out):
    rows = mm(one_hot(target[...]), got[...], 0, 0).astype(BF)
    rows_out[...] = rows
    out[...] = mm(rows, wo[...]).astype(BF)


def whole_project(target, got, wo):
    rows, cols = got.shape
    feats = wo.shape[1]
    return call(
        whole_body,
        [((rows, cols), BF), ((rows, feats), BF)],
        target,
        got,
        wo,
        flops=2 * rows * cols * (rows + feats),
    )


def out_body(target, got, wo, rows_out, other_out, mine_out):
    half = mine_out.shape[0]
    rows = mm(one_hot(target[...]), got[...], 0, 0).astype(BF)
    rows_out[...] = rows
    other_out[...] = mm(rows[half:], wo[...]).astype(BF)
    mine_out[...] = mm(rows[:half], wo[...])


def out_project(target, got, wo, *deps):
    rows, cols = got.shape
    feats = wo.shape[1]
    return call(
        out_body,
        [((rows, cols), BF), ((rows // 2, feats), BF), ((rows // 2, feats), F32)],
        target,
        got,
        wo,
        flops=2 * rows * cols * (rows + feats),
        deps=deps,
    )


def back_body(target, got, mine, other, wq, wkv, rows_out, other_out, mine_out):
    half = mine.shape[0]
    nq = wq.shape[1]
    end = nq + wkv.shape[0]
    rows = mm(one_hot(target[...]), got[:, : end + 128], 0, 0)
    coef = jnp.sum(rows[:, end:], axis=1, keepdims=True)
    low = rows[:, :end].astype(BF)
    rows_out[...] = low

    def term(part, c, held):
        value = mm(part[:, :nq], wq[...], 1, 1) + mm(part[:, nq:], wkv[...])
        return value - held[...].astype(F32) * c

    other_out[...] = term(low[half:], coef[half:], other).astype(BF)
    mine_out[...] = term(low[:half], coef[:half], mine)


def back_project(target, got, mine, other, wq, wkv):
    rows = got.shape[0]
    cols = wq.shape[1] + wkv.shape[0]
    feats = mine.shape[1]
    return call(
        back_body,
        [((rows, cols), BF), ((rows // 2, feats), BF), ((rows // 2, feats), F32)],
        target,
        got,
        mine,
        other,
        wq,
        wkv,
        flops=2 * rows * (cols + 128) * (rows + feats),
    )


def settle_body(count, got, held, out, wide_out):
    rows = held.shape[0]
    total = held[...].astype(F32)
    for i in range(count):
        total = total + got[i * rows : (i + 1) * rows].astype(F32)
    low = total.astype(BF)
    out[...] = low
    for i in range(count):
        wide_out[i * rows : (i + 1) * rows] = low


def settle(got, held):
    count = got.shape[0] // held.shape[0]
    return call(
        functools.partial(settle_body, count),
        [(held.shape, BF), (got.shape, BF)],
        got,
        held,
    )


def turn(value, cosine, sine):
    return value * cosine + pltpu.roll(value, HEAD_SIZE // 2, 1) * sine


def heads_down(value):
    count = value.shape[1] // HEAD_SIZE
    return jnp.concatenate(
        [value[:, i * HEAD_SIZE : (i + 1) * HEAD_SIZE] for i in range(count)], axis=0
    )


def heads_across(value, tokens):
    count = value.shape[0] // tokens
    return jnp.concatenate([value[i * tokens : (i + 1) * tokens] for i in range(count)], axis=1)


def add_parts(ref, tokens):
    total = ref[:tokens].astype(F32)
    for i in range(1, ref.shape[0] // tokens):
        total = total + ref[i * tokens : (i + 1) * tokens].astype(F32)
    return total


def look(total, nq, width, cosine, sine, mask):
    tokens = total.shape[0]
    heads = nq // HEAD_SIZE
    end = nq + 2 * HEAD_SIZE
    squares = jnp.sum(total[:, end:], axis=1, keepdims=True)
    scale = lax.rsqrt(squares / width + EPS)
    wide_cos = jnp.concatenate([cosine] * heads, axis=0)
    wide_sin = jnp.concatenate([sine] * heads, axis=0)
    queries = turn(heads_down(total[:, :nq] * scale), wide_cos, wide_sin).astype(BF)
    kv = (total[:, nq:end] * scale).astype(BF)
    keys = turn(kv[:, :HEAD_SIZE].astype(F32), cosine, sine).astype(BF)
    values = kv[:, HEAD_SIZE:]
    scores = mm(queries, keys, 1, 1) * (1.0 / math.sqrt(HEAD_SIZE))
    weights = jnp.exp(jnp.where(mask > 0.0, scores, -1e30))
    probs = weights / jnp.sum(weights, axis=1, keepdims=True)
    low = probs.astype(BF)
    return scale, queries, keys, values, probs, low, wide_cos, wide_sin


def look_back(total, d_mixed, nq, width, cosine, sine, seen):
    scale, queries, keys, values, probs, low, wide_cos, wide_sin = seen
    tokens = total.shape[0]
    end = nq + 2 * HEAD_SIZE
    dm = heads_down(d_mixed).astype(BF)
    d_probs = mm(dm, values, 1, 1)
    d_values = mm(low, dm, 0, 0)
    d_scores = probs * (d_probs - jnp.sum(probs * d_probs, axis=1, keepdims=True))
    d_scores = (d_scores * (1.0 / math.sqrt(HEAD_SIZE))).astype(BF)
    dq = turn(mm(d_scores, keys), wide_cos, -wide_sin)
    dk = turn(mm(d_scores, queries, 0, 0), cosine, -sine)
    dq = (heads_across(dq, tokens) * scale).astype(BF)
    dkv = (jnp.concatenate([dk, d_values], axis=1) * scale).astype(BF)
    both = jnp.concatenate([dq, dkv], axis=1)
    dot = jnp.sum(both.astype(F32) * total[:, :end], axis=1, keepdims=True)
    return jnp.concatenate([both, pair_columns(dot * scale * scale / width)], axis=1)


def spread(out, value):
    rows = value.shape[0]
    for i in range(out.shape[0] // rows):
        out[i * rows : (i + 1) * rows] = value


def forward_body(nq, width, got, cosine, sine, mask, mixed_out, total_out):
    tokens = cosine.shape[0]
    total = add_parts(got, tokens)
    total_out[...] = total
    seen = look(total, nq, width, cosine[...], sine[...], mask[...])
    spread(mixed_out, heads_across(mm(seen[5], seen[3]), tokens).astype(BF))


def both_body(nq, width, got, cosine, sine, mask, sent_out):
    tokens = cosine.shape[0]
    total = add_parts(got, tokens)
    d_mixed = total[:, total.shape[1] - nq :]
    total = total[:, : total.shape[1] - nq]
    seen = look(total, nq, width, cosine[...], sine[...], mask[...])
    mixed = heads_across(mm(seen[5], seen[3]), tokens).astype(BF)
    sent = look_back(total, d_mixed, nq, width, cosine[...], sine[...], seen)
    spread(sent_out, jnp.concatenate([sent, mixed], axis=1))


def backward_body(nq, width, total, grads, cosine, sine, mask, sent_out):
    tokens = cosine.shape[0]
    d_mixed = add_parts(grads, tokens)
    seen = look(total[...], nq, width, cosine[...], sine[...], mask[...])
    spread(sent_out, look_back(total[...], d_mixed, nq, width, cosine[...], sine[...], seen))


def shards(
    inputs,
    positions,
    out_grads,
    query_weight,
    key_value_weight,
    out_weight,
    query_stale,
    key_value_previous_gradient,
    out_stale,
):
    n_dp = lax.axis_size("dp")
    ranks = lax.axis_size("tensor")
    nz = ranks // 2
    pipe = lax.axis_index("pipe")
    rank = lax.axis_index("tensor")
    core = rank % 2
    first = pipe == 0
    micro, own, width = inputs.shape
    feats = width // n_dp
    block = own * ranks
    tokens = block * n_dp
    half = tokens // 2

    query_new = (query_weight.astype(F32) - LR * query_stale).astype(BF)
    kv_new = (key_value_weight.astype(F32) - LR * key_value_previous_gradient).astype(BF)
    out_new = (out_weight.astype(F32) - LR * out_stale).astype(BF)

    def arrange(own_part, other):
        return jnp.where(first, own_part, other), jnp.where(first, other, own_part)

    wq0, wq1 = arrange(query_new[0], swap(query_new[0], "pipe", 1))
    kv_own = kv_new[0].T
    kv_here, kv_next = arrange(kv_own, swap(kv_own, "pipe", 1))
    even = (rank // 2) % 2 == 0

    def whole_head(own_part):
        side = swap(own_part, "tensor", 1)
        pair = jnp.where(
            core == 0,
            jnp.concatenate([own_part, side], axis=0),
            jnp.concatenate([side, own_part], axis=0),
        )
        far = swap(pair, "tensor", 2)
        return jnp.where(
            even,
            jnp.concatenate([pair, far], axis=0),
            jnp.concatenate([far, pair], axis=0),
        )

    wkv0 = whole_head(kv_here)

    at = lax.broadcasted_iota(jnp.int32, (1, tokens), 1)
    inside = at % half
    chip = inside // (n_dp * own)
    rest = inside % (n_dp * own)
    target = (rest // own) * block + (chip * 2 + ((at // half) ^ core)) * own + rest % own
    rest = at % (n_dp * own)
    by_rank = (rest // own) * block + (at // (n_dp * own)) * own + rest % own

    spots = lax.dynamic_index_in_dim(positions, pipe, 0, keepdims=False)
    freqs = THETA ** (-2.0 * jnp.arange(HEAD_SIZE // 2, dtype=F32) / HEAD_SIZE)
    angles = spots.astype(F32)[:, None] * freqs[None, :]
    cosine = jnp.concatenate([jnp.cos(angles)] * 2, axis=1)
    sine = jnp.concatenate([-jnp.sin(angles), jnp.sin(angles)], axis=1)
    index = jnp.arange(block, dtype=jnp.int32)
    visible = (index[None, :] <= index[:, None]) & (index[None, :] >= (index - spots)[:, None])
    nq = query_new.shape[2]
    mask = jnp.concatenate([visible.astype(F32)] * (nq // HEAD_SIZE), axis=0)

    start = jnp.stack(
        [
            lax.dynamic_index_in_dim(inputs, pipe, 0, keepdims=False),
            lax.dynamic_index_in_dim(out_grads, pipe, 0, keepdims=False),
        ]
    )
    start = start.reshape(2, own, n_dp, feats).transpose(2, 0, 1, 3).reshape(n_dp * 2 * own, feats)
    start = dp_exchange(start).reshape(n_dp, 2, own, feats)
    h0 = start[:, 0].reshape(n_dp * own, feats)
    g1 = start[:, 1].reshape(n_dp * own, feats)

    def gather_z(tiled):
        mine = z_exchange(tiled)
        return mine, swap(mine, "tensor", 1)

    def scatter_z(part_mine, part_other):
        moved = swap(part_other, "tensor", 1)
        return z_exchange((part_mine + moved.astype(F32)).astype(BF))

    def head_rows(columns):
        return [((n_dp * block, columns), BF)]

    sent_columns = nq + 2 * HEAD_SIZE + 128

    h0_mine, h0_other = gather_z(tile_rows(h0, nz))
    part = project(target, h0_mine, h0_other, wq0, wkv0)
    part, g1_sent, own_out, kv_next = lax.optimization_barrier((part, g1, out_new[0], kv_next))
    got = dp_exchange(part)
    all_g1 = lax.all_gather(g1_sent, "tensor", axis=0, tiled=True)
    wo0, wo1 = arrange(own_out, swap(own_out, "pipe", 1))
    wkv1 = whole_head(kv_next)
    mixed0, total0 = call(
        functools.partial(forward_body, nq, width),
        head_rows(nq) + [((block, sent_columns), F32)],
        got,
        cosine,
        sine,
        mask,
    )
    got_m0, all_g1 = lax.optimization_barrier((dp_exchange(mixed0), all_g1))
    all_m0, far0, near0 = out_project(target, got_m0, wo0, wkv1)
    h1, h1_tiled = settle(scatter_z(near0, far0), h0)

    dm1 = mixed_grad(by_rank, [all_g1], wo1)
    h1_mine, h1_other = gather_z(h1_tiled)
    got = dp_exchange(project(target, h1_mine, h1_other, wq1, wkv1, dm1))
    sent1 = call(
        functools.partial(both_body, nq, width),
        head_rows(sent_columns + nq),
        got,
        cosine,
        sine,
        mask,
    )[0]
    got1 = dp_exchange(sent1)
    rows1, far1, near1 = back_project(target, got1, h1_mine, h1_other, wq1, wkv1)
    g0, g0_tiled = settle(scatter_z(near1, far1), g1)

    def section_grads(rows, mine, other):
        grad_q = mm(mine, rows[:half, :nq], 0, 0) + mm(other, rows[half:, :nq], 0, 0)
        grad_kv = mm(rows[:half, nq:], mine, 0, 0) + mm(rows[half:, nq:], other, 0, 0)
        return grad_q, grad_kv

    g0_mine, g0_other = gather_z(g0_tiled)
    gq1, gkv1 = section_grads(rows1, h1_mine, h1_other)
    all_m1, term1 = whole_project(by_rank, got1[:, sent_columns:], wo1)
    go1 = mm(all_m1, all_g1, 0, 0)
    out1 = lax.psum_scatter(term1, "tensor", scatter_dimension=0, tiled=True)
    h2 = (h1.astype(F32) + out1.astype(F32)).astype(BF)
    got_dm0 = dp_exchange(mixed_grad(target, [g0_mine, g0_other], wo0))
    sent0 = call(
        functools.partial(backward_body, nq, width),
        head_rows(sent_columns),
        total0,
        got_dm0,
        cosine,
        sine,
        mask,
    )[0]
    go0 = mm(all_m0[:half], g0_mine, 0, 0) + mm(all_m0[half:], g0_other, 0, 0)
    rows0, far, near = back_project(target, dp_exchange(sent0), h0_mine, h0_other, wq0, wkv0)
    gi, _ = settle(scatter_z(near, far), g0)
    gq0, gkv0 = section_grads(rows0, h0_mine, h0_other)

    def kv_columns(grad):
        cols = grad.shape[0] // 4
        quarters = grad.astype(BF).reshape(2, 2, cols, feats)
        keep = lax.dynamic_index_in_dim(quarters, core, 1, keepdims=False)
        send = lax.dynamic_index_in_dim(quarters, 1 - core, 1, keepdims=False)
        pair = keep.astype(F32) + swap(send, "tensor", 1).astype(F32)
        pair = pair.astype(BF)
        zz = (rank // 2) % 2
        keep = lax.dynamic_index_in_dim(pair, zz, 0, keepdims=False)
        send = lax.dynamic_index_in_dim(pair, 1 - zz, 0, keepdims=False)
        return keep.astype(F32) + swap(send, "tensor", 2).astype(F32)

    def home(grad0, grad1):
        to1 = lax.ppermute(grad1.astype(BF), "pipe", [(0, 1)])
        to0 = lax.ppermute(grad0.astype(BF), "pipe", [(1, 0)])
        return jnp.where(first, grad0 + to0.astype(F32), grad1 + to1.astype(F32))

    query_grad = home(gq0, gq1)
    kv_grad = home(kv_columns(gkv0), kv_columns(gkv1)).T
    out_grad = home(go0, go1)

    ends = jnp.stack([h1, gi, h2, g0]).reshape(2, 2, n_dp, own, feats).transpose(2, 0, 1, 3, 4)
    ends = lax.all_to_all(
        ends.reshape(n_dp * 4 * own, feats), ("dp", "pipe"), 0, 0, tiled=True
    ).reshape(n_dp, micro, 2, own, feats)
    rows = ends.transpose(2, 1, 3, 0, 4).reshape(2, micro, own, width)
    return (
        rows[0][None],
        rows[1][None],
        query_new,
        kv_new,
        out_new,
        query_grad[None],
        kv_grad[None],
        out_grad[None],
    )


def solution(mesh):
    placed = (
        P(None, ("dp", "tensor"), None),
        P(None, "dp"),
        P(None, ("dp", "tensor"), None),
        P("pipe", "dp", "tensor"),
        P("pipe", "dp", "tensor"),
        P("pipe", "tensor", "dp"),
        P("pipe", "dp", "tensor"),
        P("pipe", "dp", "tensor"),
        P("pipe", "tensor", "dp"),
    )
    return jax.shard_map(
        shards,
        mesh=mesh,
        in_specs=placed,
        out_specs=(
            P("pipe", None, ("dp", "tensor"), None),
            P("pipe", None, ("dp", "tensor"), None),
            P("pipe", "dp", "tensor"),
            P("pipe", "dp", "tensor"),
            P("pipe", "tensor", "dp"),
            P("pipe", "dp", "tensor"),
            P("pipe", "dp", "tensor"),
            P("pipe", "tensor", "dp"),
        ),
        check_vma=False,
    )
```
